32 devices in a mesh: fields: 2 (over y), rows: 4 (over z), cols: 2 (over x), sub: 2 (over core).
Axes of the slice: x: 2, y: 2, z: 4, core: 2. Of those that a mesh axis runs over, the one named last changes fastest.
Arguments:
- convergence: bfloat16 [32, 32, 16, 512], P(('fields', 'rows'), 'cols'), parts along dimension 0, may hold values from -6 to 6
- block_level: int32 [32, 32], P(('fields', 'rows'), 'cols'), parts along dimension 0, may hold values from 0 to 1
- near_codes: int32 [32, 32, 8], P(('fields', 'rows'), 'cols', 'sub'), parts along dimension 0, may hold values from 0 to 24, as said below
- far_rows: int32 [32, 32, 4], P(('fields', 'rows'), 'cols', 'sub'), parts along dimension 0, may hold values from 0 to 15, as said below
- near_factor: bfloat16 [512, 4096], P(None, 'sub'), may hold values from -0.09375 to 0.09375
- far_factor: bfloat16 [512, 2048], P(None, 'sub'), may hold values from -0.125 to 0.125
Outputs:
- whitened: bfloat16 [32, 32, 16, 512], P(('fields', 'rows'), 'cols', 'sub'), parts along dimension 0
The draws below stay inside these ranges and needn't reach their ends.
There are 2 independent parts, one for each index of `fields`. The reference program is written for one: setup_inputs(seed, part) draws one part's arguments, and reference() takes and returns one part's arrays. A program takes and returns all parts, laid end to end along the dimension named above; an argument that names none is the same for every part. Nothing has to cross between parts.
Inputs may be any that keep to these rules, and one draw needn't show every extreme that they name: `near_codes`: the 8 codes of a block are different from one another and never 12 (the block itself). `far_rows`: an entry never names a block row held by the same index of rows as the block. Among the 128 entries that one index of rows, cols and sub holds (slots 0 to 1 or 2 to 3), each other index of rows is named at most 64 times through its block rows, and one is named exactly 64 times.
All inputs are finite; a program needn't handle non-finite values.
Results may differ from the reference program's by a relative error of at most 0.001.
Values may be sent and summed in bfloat16 or wider, within the bound.
No kernel may reach another device: no remote copies, remote signals or barrier semaphores. Data moves between devices by JAX's collectives and lax.ppermute only.
A program may use at most 64 MiB of HBM per device.

```python
import jax
import jax.numpy as jnp
from jax import lax

PIX = 512
NEAR = 8
FAR = 4
SAMPLES = 16
TILE_ROWS = 4
TILE_COLS = 16
BROWS = 16
BCOLS = 32
CAP = 64
N_ROWS = 4
N_COLS = 2


def draw_near_codes(key, part):
    scores = jax.random.randint(key, (BROWS, BCOLS, 24), 0, 2 ** 20) * 32 + jnp.arange(24, dtype=jnp.int32)
    ranked = jnp.argsort(scores, axis=-1)[..., :NEAR]
    return (ranked + (ranked >= 12)).astype(jnp.int32)


def draw_far_rows(key, part):
    group_count = N_ROWS * N_COLS * 2
    per_group = 2 * TILE_ROWS * TILE_COLS
    group_keys = jax.random.split(key, group_count)

    def draw_group(group_key, group_index):
        own_row = group_index // (N_COLS * 2)
        key_hot, key_pool, key_mix, key_inner = jax.random.split(group_key, 4)
        hot_source = jax.random.randint(key_hot, (), 0, N_ROWS - 1)
        spare_pool = jnp.arange((N_ROWS - 2) * CAP, dtype=jnp.int32) // CAP
        spare_pool = spare_pool + (spare_pool >= hot_source)
        spare_pool = jax.random.permutation(key_pool, spare_pool)[:per_group - CAP]
        chosen = jnp.concatenate([jnp.zeros((CAP,), jnp.int32) + hot_source, spare_pool])
        chosen = jax.random.permutation(key_mix, chosen)
        device = chosen + (chosen >= own_row)
        row_within = jax.random.randint(key_inner, (per_group,), 0, TILE_ROWS)
        return (device * TILE_ROWS + row_within).astype(jnp.int32)
    drawn = jax.vmap(draw_group)(group_keys, jnp.arange(group_count, dtype=jnp.int32))
    drawn = drawn.reshape(N_ROWS, N_COLS, 2, TILE_ROWS, TILE_COLS, 2)
    drawn = jnp.transpose(drawn, (0, 3, 1, 4, 2, 5))
    return drawn.reshape(BROWS, BCOLS, FAR).astype(jnp.int32)


def plant(array, stream_key, smallest, high):
    longest = array.shape.index(max(array.shape))
    spots = []
    for shift in (0, 1):
        where = [jax.random.randint(jax.random.fold_in(stream_key, axis), (), 0, length) for axis, length in enumerate(array.shape)]
        where[longest] = (where[longest] + shift) % array.shape[longest]
        spots.append(tuple(where))
    return array.at[spots[0]].set(smallest).at[spots[1]].set(high)


def shard_levels(own_key, shape, cuts, smallest, high):
    level = 1.0
    for dim, shards_of in cuts:
        steps = jax.random.uniform(jax.random.fold_in(jax.random.fold_in(own_key, 6), dim), (shards_of,), jnp.float32, smallest / len(cuts), high / len(cuts))
        level = level * jnp.repeat(jnp.exp(steps), shape[dim] // shards_of).reshape((-1,) + (1,) * (len(shape) - 1 - dim))
    return level


def scatter_about(rng, shape, scale, reach, cuts=(), held_as=jnp.bfloat16):
    array = jax.random.normal(rng, shape, jnp.float32) * scale
    if len(cuts) > 0:
        array = shard_levels(rng, shape, cuts, -0.22, 0.18) * array
    return jnp.clip(array, min=-reach, max=reach).astype(held_as)


def setup_inputs(seed: int = 0, part: int = 0) -> dict:
    key_of = jax.random.split(jax.random.key(seed), 7)
    part_keys = jax.random.split(jax.random.fold_in(key_of[6], part), 7)
    convergence = scatter_about(part_keys[0], (BROWS, BCOLS, SAMPLES, PIX), 1.0, 6.0, ((0, 4), (1, 2)))
    block_level = plant(jax.random.randint(part_keys[1], (BROWS, BCOLS), 0, 2), jax.random.fold_in(part_keys[1], 1), 0, 1).astype(jnp.int32)
    near_codes = draw_near_codes(jax.random.fold_in(jax.random.fold_in(key_of[6], part), 71), part)
    far_rows = draw_far_rows(jax.random.fold_in(jax.random.fold_in(key_of[6], part), 71), part)
    near_factor = scatter_about(key_of[4], (PIX, NEAR * PIX), (NEAR * PIX) ** -0.5, 0.09375, ((1, 2),))
    far_factor = scatter_about(key_of[5], (PIX, FAR * PIX), (FAR * PIX) ** -0.5, 0.125, ((1, 2),))
    return {"convergence": convergence, "block_level": block_level, "near_codes": near_codes, "far_rows": far_rows, "near_factor": near_factor, "far_factor": far_factor}


def reference(convergence, block_level, near_codes, far_rows, near_factor, far_factor):
    padded = jnp.pad(convergence, ((2, 2), (2, 2), (0, 0), (0, 0)))
    near_weight = near_factor.astype(jnp.float32).reshape(PIX, NEAR, PIX)
    far_weight = far_factor.astype(jnp.float32).reshape(PIX, FAR, PIX)
    columns = jnp.arange(BCOLS, dtype=jnp.int32)

    def one_row(row):
        codes = near_codes[row]
        row_index = (row + codes // 5).astype(jnp.int32)
        col_index = (columns[:, None] + codes % 5).astype(jnp.int32)
        near_blocks = padded[row_index, col_index].astype(jnp.float32)
        near_term = jnp.einsum("cksq,pkq->csp", near_blocks, near_weight)
        far_blocks = convergence[far_rows[row].astype(jnp.int32), columns[:, None]].astype(jnp.float32)
        far_term = jnp.einsum("cksq,pkq->csp", far_blocks, far_weight)
        mean = jnp.where(block_level[row][:, None, None] == 1, near_term, far_term)
        return (convergence[row].astype(jnp.float32) - mean).astype(jnp.bfloat16)

    return lax.map(one_row, jnp.arange(BROWS, dtype=jnp.int32))
```

```python
import jax
import jax.numpy as jnp
from jax import lax
from jax.sharding import PartitionSpec as P

REACH = 2
CHUNKS = 2


def exchange(array, axis, parity):
    count, subs = lax.axis_size(axis), lax.axis_size("sub")
    partner = list(range(count))
    for i in range(parity, count - 1, 2):
        partner[i], partner[i + 1] = i + 1, i
    pairs = []
    for i in range(count):
        for s in range(subs):
            other = s if partner[i] != i else subs - 1 - s
            pairs.append((i * subs + s, partner[i] * subs + other))
    return lax.ppermute(array, (axis, "sub"), pairs)


def swap_sub(array):
    subs = lax.axis_size("sub")
    return lax.ppermute(array, "sub", [(s, subs - 1 - s) for s in range(subs)])


def mean_of(flat, index, factors):
    total = None
    slots = index.shape[1] // len(factors)
    for part, factor in enumerate(factors):
        chosen = index[:, part * slots : (part + 1) * slots]
        blocks = flat.at[chosen.reshape(-1)].get(mode="promise_in_bounds")
        blocks = blocks.reshape(chosen.shape + flat.shape[1:])
        term = lax.dot_general(
            blocks, factor, (((1, 3), (1, 2)), ((), ())), preferred_element_type=jnp.float32
        )
        total = term if total is None else total + term
    return total


def on_device(convergence, block_level, near_codes, far_rows, near_factor, far_factor):
    tile_rows, tile_cols, samples, pixels = convergence.shape
    rows, cols = lax.axis_size("rows"), lax.axis_size("cols")
    row, col, sub = lax.axis_index("rows"), lax.axis_index("cols"), lax.axis_index("sub")
    half = samples // lax.axis_size("sub")
    near_slots, far_slots = near_codes.shape[2], far_rows.shape[2]
    width = tile_cols // CHUNKS
    even_row, even_col = row % 2 == 0, col % 2 == 0

    own = [
        lax.dynamic_slice(
            convergence, (0, c * width, sub * half, 0), (tile_rows, width, half, pixels)
        )
        for c in range(CHUNKS)
    ]

    even = [[exchange(x, "rows", 0) for x in own]]
    odd = [[exchange(x, "rows", 1) for x in own]]
    inner = rows > 4
    for step in range(1, rows - 2):
        if inner and step < rows - 3:
            even.append([exchange(x, "rows", 0) for x in odd[step - 1]])
        odd.append([exchange(x, "rows", 1) for x in even[step - 1]])

    partner_rows = exchange(far_rows, "rows", 0)
    codes = jnp.concatenate([near_codes, far_rows, partner_rows], axis=2)
    other = swap_sub(codes)
    near_all = jnp.concatenate([near_codes, other[:, :, :near_slots]], axis=2)
    far_all = jnp.concatenate([far_rows, other[:, :, near_slots : near_slots + far_slots]], axis=2)
    partner_all = jnp.concatenate([partner_rows, other[:, :, near_slots + far_slots :]], axis=2)
    near_factors = [f.reshape(pixels, near_slots, pixels) for f in (near_factor, swap_sub(near_factor))]
    far_factors = [f.reshape(pixels, far_slots, pixels) for f in (far_factor, swap_sub(far_factor))]

    stack = jnp.concatenate(
        [jnp.concatenate(x, axis=1) for x in (own, even[0], odd[0])], axis=0
    )
    pieces = [stack]
    for parity in range(min(cols - 1, 2)):
        start = jnp.where(even_col == (parity == 0), tile_cols - REACH, 0)
        edge = lax.dynamic_slice_in_dim(stack, start, REACH, axis=1)
        pieces.append(exchange(edge, "cols", parity))
    wide = jnp.concatenate(pieces, axis=1)
    wide_cols = wide.shape[1]
    flat = wide.reshape((-1, half, pixels))
    flat = jnp.concatenate([flat, jnp.zeros((1, half, pixels), flat.dtype)], axis=0)
    at_row = jnp.arange(tile_rows, dtype=jnp.int32)[:, None, None] + near_all // 5 - REACH
    at_col = jnp.arange(tile_cols, dtype=jnp.int32)[None, :, None] + near_all % 5 - REACH
    up, down = jnp.where(even_row, 2, 1) * tile_rows, jnp.where(even_row, 1, 2) * tile_rows
    left = tile_cols + jnp.where(even_col, REACH, 0)
    right = tile_cols + jnp.where(even_col, 0, REACH)
    from_row = jnp.where(
        at_row < 0,
        up + at_row + tile_rows,
        jnp.where(at_row >= tile_rows, down + at_row - tile_rows, at_row),
    )
    from_col = jnp.where(
        at_col < 0,
        left + at_col + REACH,
        jnp.where(at_col >= tile_cols, right + at_col - tile_cols, at_col),
    )
    whole_row, whole_col = at_row + row * tile_rows, at_col + col * tile_cols
    inside = (
        (whole_row >= 0) & (whole_row < rows * tile_rows)
        & (whole_col >= 0) & (whole_col < cols * tile_cols)
    )
    near_index = jnp.where(inside, from_row * wide_cols + from_col, flat.shape[0] - 1)
    near_mean = mean_of(flat, near_index.reshape(-1, near_index.shape[2]), near_factors)
    near_mean = near_mean.reshape(tile_rows, tile_cols, half, pixels)

    shards = [own]
    place_even, place_odd = [0] * rows, [0] * rows
    for step in range(len(odd)):
        if step < len(even):
            place_even[step + 1] = len(shards)
            shards.append(even[step])
        place_odd[step + 1] = len(shards)
        shards.append(odd[step])
    place_even = jnp.array(place_even, jnp.int32)
    place_odd = jnp.array(place_odd, jnp.int32)
    source = jnp.arange(rows, dtype=jnp.int32)
    away = jnp.abs(source - row)
    by_even = (source > row) == even_row
    place = jnp.where(by_even, place_even[away], place_odd[away]) * (away > 0)

    def far_chunk(c, requests):
        flat_shards = jnp.concatenate([x[c] for x in shards], axis=0).reshape(-1, half, pixels)
        wanted = requests[:, c * width : (c + 1) * width]
        at = place[wanted // tile_rows] * tile_rows + wanted % tile_rows
        at = at * width + jnp.arange(width, dtype=jnp.int32)[None, :, None]
        mean = mean_of(flat_shards, at.reshape(-1, at.shape[2]), far_factors)
        return mean.reshape(tile_rows, width, half, pixels)

    at_end = (row == 0) | (row == rows - 1)
    done = []
    for c in range(CHUNKS):
        cols_here = slice(c * width, (c + 1) * width)
        ready = even[0][c].astype(jnp.float32) - far_chunk(c, partner_all)
        ready = exchange(ready.astype(jnp.bfloat16), "rows", 0)
        field = own[c].astype(jnp.float32)
        far_own = (field - far_chunk(c, far_all)).astype(jnp.bfloat16)
        near_own = (field - near_mean[:, cols_here]).astype(jnp.bfloat16)
        level = block_level[:, cols_here, None, None]
        done.append(jnp.where(level == 1, near_own, jnp.where(at_end, ready, far_own)))
    return jnp.concatenate(done, axis=1)


def solution(mesh):
    placed = (
        P(("fields", "rows"), "cols", None, None),
        P(("fields", "rows"), "cols"),
        P(("fields", "rows"), "cols", "sub"),
        P(("fields", "rows"), "cols", "sub"),
        P(None, "sub"),
        P(None, "sub"),
    )
    return jax.shard_map(
        on_device,
        mesh=mesh,
        in_specs=placed,
        out_specs=P(("fields", "rows"), "cols", "sub", None),
        check_vma=False,
    )
```

```python
import functools

import jax
import jax.numpy as jnp
from jax import lax
from jax.experimental import pallas as pl
from jax.experimental.pallas import tpu as pltpu
from jax.sharding import PartitionSpec as P

REACH = 2
CHUNKS = 2
VMEM_BYTES = 48 * 2**20
CONTRACT_LAST = (((1,), (1,)), ((), ()))


def exchange(array, axis, parity):
    count, subs = lax.axis_size(axis), lax.axis_size("sub")
    partner = list(range(count))
    for i in range(parity, count - 1, 2):
        partner[i], partner[i + 1] = i + 1, i
    pairs = []
    for i in range(count):
        for s in range(subs):
            other = s if partner[i] != i else subs - 1 - s
            pairs.append((i * subs + s, partner[i] * subs + other))
    return lax.ppermute(array, (axis, "sub"), pairs)


def swap_sub(array):
    subs = lax.axis_size("sub")
    return lax.ppermute(array, "sub", [(s, subs - 1 - s) for s in range(subs)])


def whole(ref_space=pltpu.VMEM):
    return pl.BlockSpec(memory_space=ref_space)


def call(kernel, rows, pixels, ints, arrays, scratch, flops):
    moved = 2 * sum(a.size for a in arrays) + 2 * rows * pixels
    return pl.pallas_call(
        kernel,
        out_shape=jax.ShapeDtypeStruct((rows, pixels), jnp.bfloat16),
        in_specs=[whole(pltpu.SMEM)] * len(ints) + [whole()] * len(arrays),
        out_specs=whole(),
        scratch_shapes=scratch,
        compiler_params=pltpu.CompilerParams(vmem_limit_bytes=VMEM_BYTES),
        cost_estimate=pl.CostEstimate(flops=flops, bytes_accessed=moved, transcendentals=0),
    )(*ints, *arrays)


def as_blocks(rows16, half):
    return rows16.astype(jnp.float32).reshape(-1, half, rows16.shape[-1])


def gather(blocks, chosen, index_of, groups, width, slots, half, pixels):
    per_step = 2 * half

    def one_group(g, carry):
        for j in range(0, width, 2):
            at = pl.multiple_of((g * width + j) * half, per_step)
            for k in range(slots):
                pair = [blocks[index_of(g, j + i, k)] for i in range(2)]
                chosen[pl.ds(at, per_step), k * pixels : (k + 1) * pixels] = (
                    jnp.concatenate(pair, axis=0).astype(jnp.bfloat16)
                )
        return carry

    lax.fori_loop(0, groups, one_group, 0)


def product(chosen, factors):
    total = None
    start = 0
    for factor in factors:
        depth = factor.shape[1]
        term = lax.dot_general(
            chosen[:, start : start + depth], factor[...], CONTRACT_LAST,
            preferred_element_type=jnp.float32,
        )
        total = term if total is None else total + term
        start += depth
    return total


def far_kernel(dims, names, position, requests, *refs):
    rows, tile_rows, width, first, half, pixels, slots = dims
    shards = refs[: len(names)]
    field, near_half, far_half, out, blocks, chosen = refs[len(names) :]
    row = position[0]
    sign = jnp.where(row % 2 == 0, 1, -1)
    count = tile_rows * width
    for (parity, step), shard in zip(names, shards):
        away = 0 if step < 0 else (1 + step) * (sign if parity == 0 else -sign)
        source = row + away
        source = jnp.where((source >= 0) & (source < rows), source, rows)
        for g in range(tile_rows):
            piece = shard[g * width * half : (g + 1) * width * half, :]
            blocks[pl.ds(source * count + g * width, width)] = as_blocks(piece, half)

    def index_of(g, j, k):
        return requests[g, first + j, k] * width + j

    gather(blocks, chosen, index_of, tile_rows, width, slots, half, pixels)
    mean = product(chosen, (near_half, far_half))
    out[...] = (field[...].astype(jnp.float32) - mean).astype(jnp.bfloat16)


def near_kernel(dims, position, index, *refs):
    rows, cols, tile_rows, tile_cols, width, half, pixels, slots = dims
    chunks = tile_cols // width
    own, even, odd = (refs[i * chunks : (i + 1) * chunks] for i in range(3))
    sides = min(cols - 1, 2)
    halos = refs[3 * chunks : 3 * chunks + sides]
    own_half, other_half, out, blocks, chosen = refs[3 * chunks + sides :]
    row, col = position[0], position[1]
    wide = tile_cols + 2 * REACH
    even_row, even_col = row % 2 == 0, col % 2 == 0
    blocks[...] = jnp.zeros_like(blocks)

    def put(at, piece):
        data = as_blocks(piece, half)
        blocks[pl.ds(at, data.shape[0])] = data

    def put_rows(refs_of, source_row, at_row, count):
        for c, ref in enumerate(refs_of):
            for g in range(count):
                begin = (source_row + g) * width * half
                put((at_row + g) * wide + REACH + c * width, ref[begin : begin + width * half, :])

    put_rows(own, 0, REACH, tile_rows)
    above, below = row > 0, row < rows - 1
    last = tile_rows - REACH

    @pl.when(above & even_row)
    def _():
        put_rows(odd, last, 0, REACH)

    @pl.when(above & jnp.logical_not(even_row))
    def _():
        put_rows(even, last, 0, REACH)

    @pl.when(below & even_row)
    def _():
        put_rows(even, 0, tile_rows + REACH, REACH)

    @pl.when(below & jnp.logical_not(even_row))
    def _():
        put_rows(odd, 0, tile_rows + REACH, REACH)

    step = REACH * half
    for parity, halo in enumerate(halos):
        on_right = even_col == (parity == 0)
        present = jnp.where(on_right, col < cols - 1, col > 0)
        at_col = jnp.where(on_right, tile_cols + REACH, 0)

        @pl.when(present)
        def _():
            for g in range(tile_rows):
                put((g + REACH) * wide + at_col, halo[g * step : (g + 1) * step, :])

        @pl.when(present & above)
        def _():
            source = jnp.where(even_row, 2, 1) * tile_rows + last
            for g in range(REACH):
                begin = pl.multiple_of((source + g) * step, step)
                put(g * wide + at_col, halo[pl.ds(begin, step), :])

        @pl.when(present & below)
        def _():
            source = jnp.where(even_row, 1, 2) * tile_rows
            for g in range(REACH):
                begin = pl.multiple_of((source + g) * step, step)
                put((tile_rows + REACH + g) * wide + at_col, halo[pl.ds(begin, step), :])

    def index_of(g, j, k):
        return index[g, j, k]

    gather(blocks, chosen, index_of, tile_rows, tile_cols, slots, half, pixels)
    mean = product(chosen, (own_half, other_half))
    for g in range(tile_rows):
        for c in range(chunks):
            at = (g * tile_cols + c * width) * half
            field = own[c][g * width * half : (g + 1) * width * half, :]
            value = field.astype(jnp.float32) - mean[at : at + width * half, :]
            out[at : at + width * half, :] = value.astype(jnp.bfloat16)


def on_device(convergence, block_level, near_codes, far_rows, near_factor, far_factor):
    tile_rows, tile_cols, samples, pixels = convergence.shape
    rows, cols = lax.axis_size("rows"), lax.axis_size("cols")
    row, col, sub = lax.axis_index("rows"), lax.axis_index("cols"), lax.axis_index("sub")
    half = samples // lax.axis_size("sub")
    near_slots, far_slots = near_codes.shape[2], far_rows.shape[2]
    width = tile_cols // CHUNKS
    position = jnp.stack([row, col]).astype(jnp.int32)

    own = [
        lax.dynamic_slice(
            convergence, (0, c * width, sub * half, 0), (tile_rows, width, half, pixels)
        ).reshape(-1, pixels)
        for c in range(CHUNKS)
    ]

    even = [[exchange(x, "rows", 0) for x in own]]
    odd = [[exchange(x, "rows", 1) for x in own]]
    inner = rows > 4
    for step in range(1, rows - 2):
        if inner and step < rows - 3:
            even.append([exchange(x, "rows", 0) for x in odd[step - 1]])
        odd.append([exchange(x, "rows", 1) for x in even[step - 1]])

    partner_rows = exchange(far_rows, "rows", 0)
    codes = jnp.concatenate([near_codes, far_rows, partner_rows], axis=2)
    other = swap_sub(codes)
    near_all = jnp.concatenate([near_codes, other[:, :, :near_slots]], axis=2)
    far_all = jnp.concatenate([far_rows, other[:, :, near_slots : near_slots + far_slots]], axis=2)
    partner_all = jnp.concatenate([partner_rows, other[:, :, near_slots + far_slots :]], axis=2)
    near_other, far_other = swap_sub(near_factor), swap_sub(far_factor)

    wide = tile_cols + 2 * REACH
    at_row = jnp.arange(tile_rows, dtype=jnp.int32)[:, None, None] + near_all // 5
    at_col = jnp.arange(tile_cols, dtype=jnp.int32)[None, :, None] + near_all % 5
    near_index = at_row * wide + at_col
    halos = []
    for parity in range(min(cols - 1, 2)):
        from_last = (col % 2 == 0) == (parity == 0)
        edge = []
        for source in (own, even[0], odd[0]):
            shaped = [x.reshape(tile_rows, width, half, pixels) for x in source]
            edge.append(jnp.where(from_last, shaped[-1][:, width - REACH :], shaped[0][:, :REACH]))
        edge = jnp.concatenate(edge, axis=0).reshape(-1, pixels)
        halos.append(exchange(edge, "cols", parity))
    tile = tile_rows * tile_cols * half
    near_depth = 2 * near_slots * pixels
    dims = (rows, cols, tile_rows, tile_cols, width, half, pixels, 2 * near_slots)
    near_own = call(
        functools.partial(near_kernel, dims),
        tile, pixels, [position, near_index],
        [*own, *even[0], *odd[0], *halos, near_factor, near_other],
        [
            pltpu.VMEM(((tile_rows + 2 * REACH) * wide, half, pixels), jnp.float32),
            pltpu.VMEM((tile, near_depth), jnp.bfloat16),
        ],
        2 * tile * near_depth * pixels,
    ).reshape(tile_rows, tile_cols, half, pixels)

    names = [(0, -1)]
    shards = [own]
    for step in range(len(odd)):
        if step < len(even):
            names.append((0, step))
            shards.append(even[step])
        names.append((1, step))
        shards.append(odd[step])

    def far_chunk(c, requests, field):
        dims = (rows, tile_rows, width, c * width, half, pixels, 2 * far_slots)
        here = tile_rows * width
        depth = 2 * far_slots * pixels
        return call(
            functools.partial(far_kernel, dims, names),
            here * half, pixels, [position, requests],
            [*(x[c] for x in shards), field, far_factor, far_other],
            [
                pltpu.VMEM(((rows + 1) * here, half, pixels), jnp.float32),
                pltpu.VMEM((here * half, depth), jnp.bfloat16),
            ],
            2 * here * half * depth * pixels,
        )

    at_end = (row == 0) | (row == rows - 1)
    done = []
    for c in range(CHUNKS):
        ready = exchange(far_chunk(c, partner_all, even[0][c]), "rows", 0)
        far_own = far_chunk(c, far_all, own[c])
        far = jnp.where(at_end, ready, far_own).reshape(tile_rows, width, half, pixels)
        level = block_level[:, c * width : (c + 1) * width, None, None]
        done.append(jnp.where(level == 1, near_own[:, c * width : (c + 1) * width], far))
    return jnp.concatenate(done, axis=1)


def solution(mesh):
    placed = (
        P(("fields", "rows"), "cols", None, None),
        P(("fields", "rows"), "cols"),
        P(("fields", "rows"), "cols", "sub"),
        P(("fields", "rows"), "cols", "sub"),
        P(None, "sub"),
        P(None, "sub"),
    )
    return jax.shard_map(
        on_device,
        mesh=mesh,
        in_specs=placed,
        out_specs=P(("fields", "rows"), "cols", "sub", None),
        check_vma=False,
    )
```

```python
import functools

import jax
import jax.numpy as jnp
from jax import lax
from jax.experimental import pallas as pl
from jax.experimental.pallas import tpu as pltpu
from jax.sharding import PartitionSpec as P

REACH = 2
PARTS = (1, 1)
VMEM_BYTES = 48 * 2**20
CONTRACT_LAST = (((1,), (1,)), ((), ()))


def exchange(array, axis, parity):
    count, subs = lax.axis_size(axis), lax.axis_size("sub")
    partner = list(range(count))
    for i in range(parity, count - 1, 2):
        partner[i], partner[i + 1] = i + 1, i
    pairs = []
    for i in range(count):
        for s in range(subs):
            other = s if partner[i] != i else subs - 1 - s
            pairs.append((i * subs + s, partner[i] * subs + other))
    return lax.ppermute(array, (axis, "sub"), pairs)


def swap_sub(array):
    subs = lax.axis_size("sub")
    return lax.ppermute(array, "sub", [(s, subs - 1 - s) for s in range(subs)])


def after(arrays, *first):
    return lax.optimization_barrier((tuple(arrays), first))[0]


def call(kernel, rows, pixels, ints, arrays, scratch, outputs=1):
    shape = jax.ShapeDtypeStruct((rows, pixels), jnp.bfloat16)
    vmem, smem = (pl.BlockSpec(memory_space=space) for space in (pltpu.VMEM, pltpu.SMEM))
    return pl.pallas_call(
        kernel,
        out_shape=[shape] * outputs,
        in_specs=[smem] * len(ints) + [vmem] * len(arrays),
        out_specs=[vmem] * outputs,
        scratch_shapes=scratch,
        compiler_params=pltpu.CompilerParams(vmem_limit_bytes=VMEM_BYTES),
    )(*ints, *arrays)


class Tile:
    def __init__(self, rows, cols, tile_rows, tile_cols, half, pixels):
        self.rows, self.cols = rows, cols
        self.tile_rows, self.tile_cols = tile_rows, tile_cols
        self.half, self.pixels = half, pixels
        self.split = tile_rows // 2
        self.units = tile_cols // REACH
        self.group = REACH * half
        self.unit = self.split * self.group
        self.wide = tile_cols + 2 * REACH

    def read(self, pieces, flag, row, unit, g):
        at = unit * self.unit + (g % self.split) * self.group
        first, second = (p[at : at + self.group, :].astype(jnp.float32) for p in pieces)
        later = row % 2 == flag
        return jnp.where(later, *((first, second) if g >= self.split else (second, first)))

    def blocks(self, value):
        return value.reshape(REACH, self.half, self.pixels)

    def gather(self, blocks, chosen, base, index_of, units, slots):
        def one_row(g, carry):
            for unit in range(units):
                at = pl.multiple_of(base + (unit * self.tile_rows + g) * self.group, self.group)
                for k in range(slots):
                    pair = [blocks[index_of(g, unit * REACH + i, k)] for i in range(REACH)]
                    chosen[pl.ds(at, self.group), k * self.pixels : (k + 1) * self.pixels] = (
                        jnp.concatenate(pair, axis=0).astype(jnp.bfloat16)
                    )
            return carry

        lax.fori_loop(0, self.tile_rows, one_row, 0)


def product(chosen, factors):
    total = None
    start = 0
    for factor in factors:
        depth = factor.shape[1]
        term = lax.dot_general(
            chosen[:, start : start + depth], factor[...], CONTRACT_LAST,
            preferred_element_type=jnp.float32,
        )
        total = term if total is None else total + term
        start += depth
    return total


def far_kernel(tile, names, first, units, wanted, slots, ints, *refs):
    row = lax.axis_index("rows")
    sign = jnp.where(row % 2 == 0, 1, -1)
    width = units * REACH
    shards = {}
    taken = 0
    for name, flag, start in names[:-1]:
        shards[name] = (refs[taken : taken + 2], flag, start)
        taken += 2
    size = units * tile.unit
    pieces = [refs[taken].at[pl.ds(at, size), :] for at in (0, size)]
    shards[names[-1][0]] = (pieces, *names[-1][1:])
    taken += 1
    own_half, other_half, *outs = refs[taken : taken + 2 + len(wanted)]
    blocks, chosen = refs[taken + 2 + len(wanted) :]
    for (parity, step), (pieces, flag, start) in shards.items():
        away = 0 if step < 0 else (1 + step) * (sign if parity == 0 else -sign)
        source = row + away
        source = jnp.where((source >= 0) & (source < tile.rows), source, tile.rows)
        for half, piece in enumerate(pieces):
            later = (row % 2 == flag) == (half == 0)
            base = source * tile.tile_rows + jnp.where(later, tile.split, 0)
            for unit in range(units):
                for g in range(tile.split):
                    at = (unit + first - start) * tile.unit + g * tile.group
                    value = piece[at : at + tile.group, :].astype(jnp.float32)
                    blocks[pl.ds((base + g) * width + unit * REACH, REACH)] = tile.blocks(value)

    count = tile.tile_rows * units * tile.group
    for n, (plane, _) in enumerate(wanted):

        def index_of(g, j, k):
            return ints[g, plane[k], first * REACH + j] * width + j

        tile.gather(blocks, chosen, n * count, index_of, units, 2 * slots)
    mean = product(chosen, (own_half, other_half))
    for n, (_, name) in enumerate(wanted):
        pieces, flag, start = shards[name]
        for unit in range(units):
            for g in range(tile.tile_rows):
                at = (unit * tile.tile_rows + g) * tile.group
                field = tile.read(pieces, flag, row, unit + first - start, g)
                value = field - mean[n * count + at : n * count + at + tile.group, :]
                outs[n][at : at + tile.group, :] = value.astype(jnp.bfloat16)


def halo(tile, row, even, odd, unit, r):
    above = r < REACH
    g = (tile.split - REACH + r) if above else (r - REACH - tile.tile_rows)
    at = unit * tile.unit + g * tile.group
    from_even, from_odd = (p[at : at + tile.group, :].astype(jnp.float32) for p in (even, odd))
    return jnp.where((row % 2 == 0) == above, from_odd, from_even)


def edge_kernel(tile, parity, first, second, even, odd, out):
    row, col = lax.axis_index("rows"), lax.axis_index("cols")
    for r in range(tile.tile_rows + 2 * REACH):
        sides = []
        for unit in (0, tile.units - 1):
            g = r - REACH
            if 0 <= g < tile.tile_rows:
                sides.append(tile.read((first, second), 0, row, unit, g))
            else:
                sides.append(halo(tile, row, even, odd, unit, r))
        value = jnp.where(col % 2 == parity, sides[1], sides[0])
        out[r * tile.group : (r + 1) * tile.group, :] = value.astype(jnp.bfloat16)


def near_kernel(tile, slots, sides, ints, first, second, even, odd, *refs):
    halos = refs[:sides]
    own_half, other_half, out, blocks, chosen = refs[sides:]
    row, col = lax.axis_index("rows"), lax.axis_index("cols")
    above, below = row > 0, row < tile.rows - 1
    wide, last = tile.wide, tile.tile_rows + REACH
    nothing = jnp.zeros((REACH, tile.half, tile.pixels), jnp.float32)
    for r in range(last + REACH):
        inside = above if r < REACH else below if r >= last else None
        for unit in range(tile.units):
            if inside is None:
                value = tile.read((first, second), 0, row, unit, r - REACH)
            else:
                value = jnp.where(inside, halo(tile, row, even, odd, unit, r), 0.0)
            blocks[pl.ds(r * wide + REACH + unit * REACH, REACH)] = tile.blocks(value)
        left, right = nothing, nothing
        for parity in range(sides):
            value = halos[parity][r * tile.group : (r + 1) * tile.group, :].astype(jnp.float32)
            if inside is not None:
                value = jnp.where(inside, value, 0.0)
            value = tile.blocks(value)
            on_right = col % 2 == parity
            right = jnp.where(on_right & (col < tile.cols - 1), value, right)
            left = jnp.where(jnp.logical_not(on_right) & (col > 0), value, left)
        blocks[pl.ds(r * wide, REACH)] = left
        blocks[pl.ds(r * wide + REACH + tile.tile_cols, REACH)] = right

    def index_of(g, j, k):
        return ints[g, k, j]

    tile.gather(blocks, chosen, 0, index_of, tile.units, 2 * slots)
    mean = product(chosen, (own_half, other_half))
    for unit in range(tile.units):
        for g in range(tile.tile_rows):
            at = (unit * tile.tile_rows + g) * tile.group
            value = tile.read((first, second), 0, row, unit, g) - mean[at : at + tile.group, :]
            out[at : at + tile.group, :] = value.astype(jnp.bfloat16)


def pick_kernel(tile, parts, level, near, *refs):
    ready, own, out = refs[: len(parts)], refs[len(parts) : 2 * len(parts)], refs[-1]
    row = lax.axis_index("rows")
    at_end = (row == 0) | (row == tile.rows - 1)
    lower = lax.broadcasted_iota(jnp.int32, (tile.group, tile.pixels), 0) // tile.half
    first = 0
    for c, units in enumerate(parts):
        for unit in range(units):
            for g in range(tile.tile_rows):
                at = (unit * tile.tile_rows + g) * tile.group
                far = [x[c][at : at + tile.group, :].astype(jnp.float32) for x in (ready, own)]
                far = jnp.where(at_end, *far)
                at = ((first + unit) * tile.tile_rows + g) * tile.group
                fine = near[at : at + tile.group, :].astype(jnp.float32)
                levels = level[g, (first + unit) * REACH]
                for i in range(1, REACH):
                    levels = jnp.where(lower == i, level[g, (first + unit) * REACH + i], levels)
                at = (g * tile.units + first + unit) * tile.group
                out[at : at + tile.group, :] = jnp.where(levels == 1, fine, far).astype(jnp.bfloat16)
        first += units


def on_device(convergence, block_level, near_codes, far_rows, near_factor, far_factor):
    tile_rows, tile_cols, samples, pixels = convergence.shape
    rows, cols = lax.axis_size("rows"), lax.axis_size("cols")
    row, sub = lax.axis_index("rows"), lax.axis_index("sub")
    half = samples // lax.axis_size("sub")
    near_slots, far_slots = near_codes.shape[2], far_rows.shape[2]
    tile = Tile(rows, cols, tile_rows, tile_cols, half, pixels)
    parts = [tile.units * part // sum(PARTS) for part in PARTS]
    starts = [sum(parts[:c]) for c in range(len(parts))]

    own = []
    for later in (row % 2 == 0, row % 2 != 0):
        start = jnp.where(later, tile.split, 0)
        piece = lax.dynamic_slice(
            convergence, (start, 0, sub * half, 0), (tile.split, tile_cols, half, pixels)
        ).reshape(tile.split, tile.units, REACH, half, pixels)
        own.append(jnp.transpose(piece, (1, 0, 2, 3, 4)).reshape(-1, pixels))

    requests = jnp.transpose(far_rows, (0, 2, 1))
    partners = exchange(requests, "rows", 0)
    far_other = swap_sub(far_factor)
    near_other = swap_sub(near_factor)

    first = exchange(own[0], "rows", 0)
    side = exchange(own[1], "rows", 1)
    held = after(own, partners, far_other, near_other)
    even = [[first, exchange(held[1], "rows", 0)]]
    odd = [[side, exchange(held[0], "rows", 1)]]

    beside = [*own, even[0][0], odd[0][0]]
    edges = [
        call(
            functools.partial(edge_kernel, tile, parity),
            (tile_rows + 2 * REACH) * tile.group, pixels, [], beside, [],
        )[0]
        for parity in range(min(cols - 1, 2))
    ]
    halos = [exchange(edge, "cols", parity) for parity, edge in enumerate(edges)]

    near_index = jnp.transpose(near_codes, (0, 2, 1))
    near_index = near_index + (tile.wide - 2 * REACH - 1) * (near_index // (2 * REACH + 1))
    near_index = near_index + tile.wide * jnp.arange(tile_rows, dtype=jnp.int32)[:, None, None]
    near_index = near_index + jnp.arange(tile_cols, dtype=jnp.int32)[None, None, :]
    codes = jnp.concatenate([near_index, requests, partners], axis=1)
    other = swap_sub(codes)
    near_ints = jnp.concatenate([near_index, other[:, :near_slots]], axis=1)
    far_ints = jnp.concatenate([codes[:, near_slots:], other[:, near_slots:]], axis=1)

    inner = rows > 4
    for step in range(1, rows - 3):
        if inner:
            even.append([exchange(x, "rows", 0) for x in odd[step - 1]])
        odd.append([exchange(x, "rows", 1) for x in even[step - 1]])
    source = after(even[rows - 4], near_ints, far_ints, *halos)
    last = []
    for start, units in zip(starts, parts):
        spots = slice(start * tile.unit, (start + units) * tile.unit)
        last.append(exchange(jnp.concatenate([x[spots] for x in source], axis=0), "rows", 1))

    size = tile_rows * tile_cols * half
    (near_own,) = call(
        functools.partial(near_kernel, tile, near_slots, len(halos)),
        size, pixels, [near_ints], [*beside, *halos, near_factor, near_other],
        [
            pltpu.VMEM(((tile_rows + 2 * REACH) * tile.wide, half, pixels), jnp.float32),
            pltpu.VMEM((size, 2 * near_slots * pixels), jnp.bfloat16),
        ],
    )

    def far_chunk(c, wanted, *before):
        names, arrays = [((0, -1), 0, 0)], [*own]
        for step in range(len(odd)):
            if step < len(even):
                names.append(((0, step), 1, 0))
                arrays += even[step]
            names.append(((1, step), 0, 0))
            arrays += odd[step]
        final = len(odd)
        names.append(((1, final), 0, starts[c]))
        arrays.append(last[c])
        if before:
            arrays = list(after(arrays[:1], *before)) + arrays[1:]
        here = tile_rows * parts[c] * tile.group
        return call(
            functools.partial(far_kernel, tile, names, starts[c], parts[c], wanted, far_slots),
            here, pixels, [far_ints], [*arrays, far_factor, far_other],
            [
                pltpu.VMEM(((rows + 1) * tile_rows * parts[c] * REACH, half, pixels), jnp.float32),
                pltpu.VMEM((len(wanted) * here, 2 * far_slots * pixels), jnp.bfloat16),
            ],
            len(wanted),
        )

    slots = [k + 2 * far_slots * s for s in range(2) for k in range(far_slots)]
    partner = ([far_slots + k for k in slots], (0, 0))
    mine = (slots, (0, -1))
    ready, far_own = [], []
    sent = near_own
    for c in range(len(parts)):
        if c < len(parts) - 1:
            sent, kept = far_chunk(c, [partner, mine], sent)
        else:
            (sent,) = far_chunk(c, [partner], sent)
            (kept,) = far_chunk(c, [mine])
        ready.append(exchange(sent, "rows", 0))
        far_own.append(kept)
    (result,) = call(
        functools.partial(pick_kernel, tile, parts),
        size, pixels, [block_level], [near_own, *ready, *far_own], [],
    )
    return result.reshape(tile_rows, tile_cols, half, pixels)


def solution(mesh):
    placed = (
        P(("fields", "rows"), "cols", None, None),
        P(("fields", "rows"), "cols"),
        P(("fields", "rows"), "cols", "sub"),
        P(("fields", "rows"), "cols", "sub"),
        P(None, "sub"),
        P(None, "sub"),
    )
    return jax.shard_map(
        on_device,
        mesh=mesh,
        in_specs=placed,
        out_specs=P(("fields", "rows"), "cols", "sub", None),
        check_vma=False,
    )
```

```python
import functools

import jax
import jax.numpy as jnp
from jax import lax
from jax.experimental import pallas as pl
from jax.experimental.pallas import tpu as pltpu
from jax.sharding import PartitionSpec as P

REACH = 2
PARTS = (3, 3, 2)
VMEM_BYTES = 48 * 2**20
CONTRACT_LAST = (((1,), (1,)), ((), ()))


def exchange(array, axis, parity):
    count, subs = lax.axis_size(axis), lax.axis_size("sub")
    partner = list(range(count))
    for i in range(parity, count - 1, 2):
        partner[i], partner[i + 1] = i + 1, i
    pairs = []
    for i in range(count):
        for s in range(subs):
            other = s if partner[i] != i else subs - 1 - s
            pairs.append((i * subs + s, partner[i] * subs + other))
    return lax.ppermute(array, (axis, "sub"), pairs)


def swap_sub(array):
    subs = lax.axis_size("sub")
    return lax.ppermute(array, "sub", [(s, subs - 1 - s) for s in range(subs)])


def after(arrays, *first):
    return lax.optimization_barrier((tuple(arrays), first))[0]


def call(kernel, rows, pixels, ints, arrays, scratch, outputs=1, left=0):
    shape = jax.ShapeDtypeStruct((rows, pixels), jnp.bfloat16)
    vmem = pl.BlockSpec(memory_space=pltpu.VMEM)
    return pl.pallas_call(
        kernel,
        out_shape=[shape] * outputs,
        in_specs=[vmem] * (len(ints) + len(arrays) - left)
        + [pl.BlockSpec(memory_space=pl.ANY)] * left,
        out_specs=[vmem] * outputs,
        scratch_shapes=scratch
        + [pltpu.SMEM(x.shape, x.dtype) for x in ints]
        + [pltpu.SemaphoreType.DMA] * len(ints),
        compiler_params=pltpu.CompilerParams(vmem_limit_bytes=VMEM_BYTES),
    )(*ints, *arrays)


class Tile:
    def __init__(self, rows, cols, tile_rows, tile_cols, half, pixels):
        self.rows, self.cols = rows, cols
        self.tile_rows, self.tile_cols = tile_rows, tile_cols
        self.half, self.pixels = half, pixels
        self.split = tile_rows // 2
        self.units = tile_cols // REACH
        self.group = REACH * half
        self.unit = self.split * self.group
        self.wide = tile_cols + 2 * REACH

    def read(self, pieces, flag, row, unit, g):
        at = unit * self.unit + (g % self.split) * self.group
        first, second = (p[at : at + self.group, :].astype(jnp.float32) for p in pieces)
        later = row % 2 == flag
        return jnp.where(later, *((first, second) if g >= self.split else (second, first)))

    def blocks(self, value):
        return value.reshape(REACH, self.half, self.pixels)

    def gather(self, blocks, chosen, base, index_of, units, slots, begin=0, count=None):
        count = self.tile_rows if count is None else count

        def one_row(g, carry):
            for unit in range(units):
                at = base + (unit * count + g - begin) * self.group
                at = pl.multiple_of(at, self.group)
                for k in range(slots):
                    pair = [blocks[index_of(g, unit * REACH + i, k)] for i in range(REACH)]
                    chosen[pl.ds(at, self.group), k * self.pixels : (k + 1) * self.pixels] = (
                        jnp.concatenate(pair, axis=0).astype(jnp.bfloat16)
                    )
            return carry

        lax.fori_loop(begin, begin + count, one_row, 0)


def product(chosen, factors):
    total = None
    start = 0
    for factor in factors:
        depth = factor.shape[1]
        term = lax.dot_general(
            chosen[:, start : start + depth], factor[...], CONTRACT_LAST,
            preferred_element_type=jnp.float32,
        )
        total = term if total is None else total + term
        start += depth
    return total


def far_kernel(tile, names, first, units, wanted, slots, ints_in, *refs):
    *refs, ints, arrived = refs
    row = lax.axis_index("rows")

    @pl.when((row > 0) & (row < tile.rows - 1))
    def _():
        copy = pltpu.make_async_copy(ints_in, ints, arrived)
        copy.start()
        sign = jnp.where(row % 2 == 0, 1, -1)
        width = units * REACH
        shards = {}
        taken = 0
        size = units * tile.unit
        for name, flag, start in names:
            if start is None:
                shards[name] = (refs[taken : taken + 2], flag, 0)
                taken += 2
            else:
                pieces = [refs[taken].at[pl.ds(at, size), :] for at in (0, size)]
                shards[name] = (pieces, flag, start)
                taken += 1
        own_half, other_half, *outs = refs[taken : taken + 2 + len(wanted)]
        blocks, chosen = refs[taken + 2 + len(wanted) :]
        for (parity, step), (pieces, flag, start) in shards.items():
            away = 0 if step < 0 else (1 + step) * (sign if parity == 0 else -sign)
            source = row + away
            source = jnp.where((source >= 0) & (source < tile.rows), source, tile.rows)
            for half, piece in enumerate(pieces):
                later = (row % 2 == flag) == (half == 0)
                base = source * tile.tile_rows + jnp.where(later, tile.split, 0)
                for unit in range(units):
                    for g in range(tile.split):
                        at = (unit + first - start) * tile.unit + g * tile.group
                        value = piece[at : at + tile.group, :].astype(jnp.float32)
                        blocks[pl.ds((base + g) * width + unit * REACH, REACH)] = tile.blocks(value)

        copy.wait()
        count = tile.tile_rows * units * tile.group
        for n, (plane, _) in enumerate(wanted):

            def index_of(g, j, k):
                return ints[g, plane[k] * tile.tile_cols + first * REACH + j] * width + j

            tile.gather(blocks, chosen, n * count, index_of, units, 2 * slots)
        mean = product(chosen, (own_half, other_half))
        for n, (_, name) in enumerate(wanted):
            pieces, flag, start = shards[name]
            for unit in range(units):
                for g in range(tile.tile_rows):
                    at = (unit * tile.tile_rows + g) * tile.group
                    field = tile.read(pieces, flag, row, unit + first - start, g)
                    value = field - mean[n * count + at : n * count + at + tile.group, :]
                    outs[n][at : at + tile.group, :] = value.astype(jnp.bfloat16)


def halo(tile, row, even, odd, unit, r):
    above = r < REACH
    g = (tile.split - REACH + r) if above else (r - REACH - tile.tile_rows)
    at = unit * tile.unit + g * tile.group
    from_even, from_odd = (p[at : at + tile.group, :].astype(jnp.float32) for p in (even, odd))
    return jnp.where((row % 2 == 0) == above, from_odd, from_even)


def edge_kernel(tile, parity, first, second, even, odd, out):
    row, col = lax.axis_index("rows"), lax.axis_index("cols")
    for r in range(tile.tile_rows + 2 * REACH):
        sides = []
        for unit in (0, tile.units - 1):
            g = r - REACH
            if 0 <= g < tile.tile_rows:
                sides.append(tile.read((first, second), 0, row, unit, g))
            else:
                sides.append(halo(tile, row, even, odd, unit, r))
        value = jnp.where(col % 2 == parity, sides[1], sides[0])
        out[r * tile.group : (r + 1) * tile.group, :] = value.astype(jnp.bfloat16)


def near_kernel(tile, slots, sides, ints_in, first, second, even, odd, *refs):
    *refs, ints, arrived = refs
    copy = pltpu.make_async_copy(ints_in, ints, arrived)
    copy.start()
    halos = refs[:sides]
    own_half, other_half, out, blocks, chosen, *factors, factor_sem = refs[sides:]
    loads = []
    for i, source in enumerate((own_half, other_half)):
        loads.append(pltpu.make_async_copy(source, factors[i], factor_sem.at[i]))
        loads[i].start()
    row, col = lax.axis_index("rows"), lax.axis_index("cols")
    above, below = row > 0, row < tile.rows - 1
    wide, last = tile.wide, tile.tile_rows + REACH
    nothing = jnp.zeros((REACH, tile.half, tile.pixels), jnp.float32)
    for r in range(last + REACH):
        inside = above if r < REACH else below if r >= last else None
        for unit in range(tile.units):
            if inside is None:
                value = tile.read((first, second), 0, row, unit, r - REACH)
            else:
                value = jnp.where(inside, halo(tile, row, even, odd, unit, r), 0.0)
            blocks[pl.ds(r * wide + REACH + unit * REACH, REACH)] = tile.blocks(value)
        left, right = nothing, nothing
        for parity in range(sides):
            value = halos[parity][r * tile.group : (r + 1) * tile.group, :].astype(jnp.float32)
            if inside is not None:
                value = jnp.where(inside, value, 0.0)
            value = tile.blocks(value)
            on_right = col % 2 == parity
            right = jnp.where(on_right & (col < tile.cols - 1), value, right)
            left = jnp.where(jnp.logical_not(on_right) & (col > 0), value, left)
        blocks[pl.ds(r * wide, REACH)] = left
        blocks[pl.ds(r * wide + REACH + tile.tile_cols, REACH)] = right

    def index_of(g, j, k):
        return ints[g, k * tile.tile_cols + j]

    copy.wait()
    tile.gather(blocks, chosen, 0, index_of, tile.units, 2 * slots)
    for load in loads:
        load.wait()
    mean = product(chosen, factors)
    for unit in range(tile.units):
        for g in range(tile.tile_rows):
            at = (unit * tile.tile_rows + g) * tile.group
            value = tile.read((first, second), 0, row, unit, g)
            out[at : at + tile.group, :] = (value - mean[at : at + tile.group, :]).astype(jnp.bfloat16)


def mix_kernel(tile, parts, level_in, near, *refs):
    *refs, level, arrived = refs
    copy = pltpu.make_async_copy(level_in, level, arrived)
    copy.start()
    copy.wait()
    own, out, awaited = refs[: len(parts)], refs[-2], refs[-1]
    row = lax.axis_index("rows")
    at_end = (row == 0) | (row == tile.rows - 1)
    lower = lax.broadcasted_iota(jnp.int32, (tile.group, tile.pixels), 0) // tile.half
    first = 0
    for c, units in enumerate(parts):
        for unit in range(units):
            for g in range(tile.tile_rows):
                at = (unit * tile.tile_rows + g) * tile.group
                far = own[c][at : at + tile.group, :].astype(jnp.float32)
                at = ((first + unit) * tile.tile_rows + g) * tile.group
                fine = near[at : at + tile.group, :].astype(jnp.float32)
                levels = level[g, (first + unit) * REACH]
                for i in range(1, REACH):
                    levels = jnp.where(lower == i, level[g, (first + unit) * REACH + i], levels)
                at = (g * tile.units + first + unit) * tile.group
                mixed = jnp.where(levels == 1, fine, far)
                out[at : at + tile.group, :] = mixed.astype(jnp.bfloat16)
                wait = jnp.where((levels != 1) & at_end, 1.0, 0.0)
                awaited[at : at + tile.group, :] = wait.astype(jnp.bfloat16)
        first += units


def final_kernel(tile, parts, mixed, awaited, *refs):
    out = refs[-1]
    first = 0
    for c, units in enumerate(parts):
        for unit in range(units):
            for g in range(tile.tile_rows):
                at = (unit * tile.tile_rows + g) * tile.group
                at_out = (g * tile.units + first + unit) * tile.group
                spot = slice(at_out, at_out + tile.group)
                far = refs[c][at : at + tile.group, :].astype(jnp.float32)
                value = mixed[spot, :].astype(jnp.float32)
                value = jnp.where(awaited[spot, :].astype(jnp.float32) > 0.5, far, value)
                out[spot, :] = value.astype(jnp.bfloat16)
        first += units


def on_device(convergence, block_level, near_codes, far_rows, near_factor, far_factor):
    tile_rows, tile_cols, samples, pixels = convergence.shape
    rows, cols = lax.axis_size("rows"), lax.axis_size("cols")
    row, sub = lax.axis_index("rows"), lax.axis_index("sub")
    half = samples // lax.axis_size("sub")
    near_slots, far_slots = near_codes.shape[2], far_rows.shape[2]
    tile = Tile(rows, cols, tile_rows, tile_cols, half, pixels)
    parts = [tile.units * part // sum(PARTS) for part in PARTS]
    starts = [sum(parts[:c]) for c in range(len(parts))]

    own = []
    for later in (row % 2 == 0, row % 2 != 0):
        start = jnp.where(later, tile.split, 0)
        piece = lax.dynamic_slice(
            convergence, (start, 0, sub * half, 0), (tile.split, tile_cols, half, pixels)
        ).reshape(tile.split, tile.units, REACH, half, pixels)
        own.append(jnp.transpose(piece, (1, 0, 2, 3, 4)).reshape(-1, pixels))

    requests = jnp.transpose(far_rows, (0, 2, 1))
    partners = exchange(requests, "rows", 0)
    far_other = swap_sub(far_factor)
    near_other = swap_sub(near_factor)

    first = exchange(own[0], "rows", 0)
    side = exchange(own[1], "rows", 1)
    held = after(own, partners, far_other, near_other)
    even = [[first, exchange(held[1], "rows", 0)]]
    odd = [[side, exchange(held[0], "rows", 1)]]

    beside = [*own, even[0][0], odd[0][0]]
    edges = [
        call(
            functools.partial(edge_kernel, tile, parity),
            (tile_rows + 2 * REACH) * tile.group, pixels, [], beside, [],
        )[0]
        for parity in range(min(cols - 1, 2))
    ]
    halos = [exchange(edge, "cols", parity) for parity, edge in enumerate(edges)]

    near_index = jnp.transpose(near_codes, (0, 2, 1))
    near_index = near_index + (tile.wide - 2 * REACH - 1) * (near_index // (2 * REACH + 1))
    near_index = near_index + tile.wide * jnp.arange(tile_rows, dtype=jnp.int32)[:, None, None]
    near_index = near_index + jnp.arange(tile_cols, dtype=jnp.int32)[None, None, :]
    codes = jnp.concatenate([near_index, requests, partners], axis=1)
    other = swap_sub(codes)
    near_ints = jnp.concatenate([near_index, other[:, :near_slots]], axis=1)
    far_ints = jnp.concatenate([codes[:, near_slots:], other[:, near_slots:]], axis=1)
    near_ints, far_ints = (x.reshape(tile_rows, -1) for x in (near_ints, far_ints))

    size = tile_rows * tile_cols * half
    (near_own,) = call(
        functools.partial(near_kernel, tile, near_slots, len(halos)),
        size, pixels, [near_ints], [*beside, *halos, near_factor, near_other],
        [
            pltpu.VMEM(((tile_rows + 2 * REACH) * tile.wide, half, pixels), jnp.float32),
            pltpu.VMEM((size, 2 * near_slots * pixels), jnp.bfloat16),
            pltpu.VMEM(near_factor.shape, near_factor.dtype),
            pltpu.VMEM(near_factor.shape, near_factor.dtype),
            pltpu.SemaphoreType.DMA((2,)),
        ],
        left=2,
    )

    inner = rows > 4
    for step in range(1, rows - 3):
        if inner:
            even.append([exchange(x, "rows", 0) for x in odd[step - 1]])
        odd.append([exchange(x, "rows", 1) for x in even[step - 1]])
    source = after(even[rows - 4], near_ints, far_ints, *halos, odd[0][1])
    def cut(pieces, c):
        spots = slice(starts[c] * tile.unit, (starts[c] + parts[c]) * tile.unit)
        return jnp.concatenate([x[spots] for x in pieces], axis=0)

    last = [exchange(cut(source, c), "rows", 1) for c in range(len(parts))]

    def far_chunk(c, wanted, *before):
        names, arrays = [((0, -1), 0, None)], [*own]
        for step in range(len(odd)):
            if step < len(even):
                names.append(((0, step), 1, None))
                arrays += even[step]
            names.append(((1, step), 0, None))
            arrays += odd[step]
        names.append(((1, len(odd)), 0, starts[c]))
        arrays.append(last[c])
        if before:
            arrays = list(after(arrays[:1], *before)) + arrays[1:]
        here = tile_rows * parts[c] * tile.group
        return call(
            functools.partial(
                far_kernel, tile, names, starts[c], parts[c], wanted, far_slots
            ),
            here, pixels, [far_ints], [*arrays, far_factor, far_other],
            [
                pltpu.VMEM(((rows + 1) * tile_rows * parts[c] * REACH, half, pixels), jnp.float32),
                pltpu.VMEM((len(wanted) * here, 2 * far_slots * pixels), jnp.bfloat16),
            ],
            len(wanted),
        )

    slots = [k + 2 * far_slots * s for s in range(2) for k in range(far_slots)]
    partner = ([far_slots + k for k in slots], (0, 0))
    mine = (slots, (0, -1))
    ready = []
    sent = near_own
    for c in range(len(parts)):
        (sent,) = far_chunk(c, [partner], sent)
        ready.append(exchange(sent, "rows", 0))
    far_own = [far_chunk(c, [mine], sent)[0] for c in range(len(parts))]
    mixed, awaited = call(
        functools.partial(mix_kernel, tile, parts),
        size, pixels, [block_level], [near_own, *far_own], [], 2,
    )
    (result,) = call(
        functools.partial(final_kernel, tile, parts),
        size, pixels, [], [mixed, awaited, *ready], [],
    )
    return result.reshape(tile_rows, tile_cols, half, pixels)


def solution(mesh):
    placed = (
        P(("fields", "rows"), "cols", None, None),
        P(("fields", "rows"), "cols"),
        P(("fields", "rows"), "cols", "sub"),
        P(("fields", "rows"), "cols", "sub"),
        P(None, "sub"),
        P(None, "sub"),
    )
    return jax.shard_map(
        on_device,
        mesh=mesh,
        in_specs=placed,
        out_specs=P(("fields", "rows"), "cols", "sub", None),
        check_vma=False,
    )
```

```python
import functools

import jax
import jax.numpy as jnp
from jax import lax
from jax.experimental import pallas as pl
from jax.experimental.pallas import tpu as pltpu
from jax.sharding import PartitionSpec as P

REACH = 2
PARTS = (3, 3, 2)
VMEM_BYTES = 48 * 2**20
CONTRACT_LAST = (((1,), (1,)), ((), ()))


def exchange(array, axis, parity):
    count, subs = lax.axis_size(axis), lax.axis_size("sub")
    partner = list(range(count))
    for i in range(parity, count - 1, 2):
        partner[i], partner[i + 1] = i + 1, i
    pairs = []
    for i in range(count):
        for s in range(subs):
            other = s if partner[i] != i else subs - 1 - s
            pairs.append((i * subs + s, partner[i] * subs + other))
    return lax.ppermute(array, (axis, "sub"), pairs)


def swap_sub(array):
    subs = lax.axis_size("sub")
    return lax.ppermute(array, "sub", [(s, subs - 1 - s) for s in range(subs)])


def after(arrays, *first):
    return lax.optimization_barrier((tuple(arrays), first))[0]


def call(kernel, rows, pixels, ints, arrays, scratch, outputs=1, left=0, more=()):
    shape = jax.ShapeDtypeStruct((rows, pixels), jnp.bfloat16)
    vmem = pl.BlockSpec(memory_space=pltpu.VMEM)
    return pl.pallas_call(
        kernel,
        out_shape=[shape] * outputs + list(more),
        in_specs=[vmem] * (len(ints) + len(arrays) - left)
        + [pl.BlockSpec(memory_space=pltpu.HBM)] * left,
        out_specs=[vmem] * (outputs + len(more)),
        scratch_shapes=scratch
        + [pltpu.SMEM(x.shape, x.dtype) for x in ints]
        + [pltpu.SemaphoreType.DMA] * len(ints),
        compiler_params=pltpu.CompilerParams(vmem_limit_bytes=VMEM_BYTES),
    )(*ints, *arrays)


class Tile:
    def __init__(self, rows, cols, tile_rows, tile_cols, half, pixels):
        self.rows, self.cols = rows, cols
        self.tile_rows, self.tile_cols = tile_rows, tile_cols
        self.half, self.pixels = half, pixels
        self.split = tile_rows // 2
        self.units = tile_cols // REACH
        self.group = REACH * half
        self.unit = self.split * self.group
        self.wide = tile_cols + 2 * REACH

    def read(self, pieces, flag, row, unit, g):
        at = unit * self.unit + (g % self.split) * self.group
        first, second = (p[at : at + self.group, :].astype(jnp.float32) for p in pieces)
        later = row % 2 == flag
        return jnp.where(later, *((first, second) if g >= self.split else (second, first)))

    def blocks(self, value):
        return value.reshape(REACH, self.half, self.pixels)

    def gather(self, blocks, chosen, base, index_of, units, slots):
        def one_row(g, carry):
            for n, unit in enumerate(units):
                at = pl.multiple_of(base + (n * self.tile_rows + g) * self.group, self.group)
                for k in range(slots):
                    pair = [blocks[index_of(g, unit * REACH + i, k)] for i in range(REACH)]
                    chosen[pl.ds(at, self.group), k * self.pixels : (k + 1) * self.pixels] = (
                        jnp.concatenate(pair, axis=0).astype(jnp.bfloat16)
                    )
            return carry

        lax.fori_loop(0, self.tile_rows, one_row, 0)


def product(chosen, factors):
    total = None
    start = 0
    for factor in factors:
        depth = factor.shape[1]
        term = lax.dot_general(
            chosen[:, start : start + depth], factor[...], CONTRACT_LAST,
            preferred_element_type=jnp.float32,
        )
        total = term if total is None else total + term
        start += depth
    return total


def far_kernel(tile, names, first, units, wanted, slots, ints_in, *refs):
    *refs, ints, arrived = refs
    row = lax.axis_index("rows")

    @pl.when((row > 0) & (row < tile.rows - 1))
    def _():
        copy = pltpu.make_async_copy(ints_in, ints, arrived)
        copy.start()
        sign = jnp.where(row % 2 == 0, 1, -1)
        width = units * REACH
        shards = {}
        taken = 0
        size = units * tile.unit
        for name, flag, start in names:
            if start is None:
                shards[name] = (refs[taken : taken + 2], flag, 0)
                taken += 2
            else:
                pieces = [refs[taken].at[pl.ds(at, size), :] for at in (0, size)]
                shards[name] = (pieces, flag, start)
                taken += 1
        own_half, other_half, *outs = refs[taken : taken + 2 + len(wanted)]
        blocks, chosen = refs[taken + 2 + len(wanted) :]
        for (parity, step), (pieces, flag, start) in shards.items():
            away = 0 if step < 0 else (1 + step) * (sign if parity == 0 else -sign)
            source = row + away
            source = jnp.where((source >= 0) & (source < tile.rows), source, tile.rows)
            for half, piece in enumerate(pieces):
                later = (row % 2 == flag) == (half == 0)
                base = source * tile.tile_rows + jnp.where(later, tile.split, 0)
                for unit in range(units):
                    for g in range(tile.split):
                        at = (unit + first - start) * tile.unit + g * tile.group
                        value = piece[at : at + tile.group, :].astype(jnp.float32)
                        blocks[pl.ds((base + g) * width + unit * REACH, REACH)] = tile.blocks(value)

        copy.wait()
        count = tile.tile_rows * units * tile.group
        for n, (plane, _) in enumerate(wanted):

            def index_of(g, j, k):
                return ints[g, plane[k] * tile.tile_cols + first * REACH + j] * width + j

            tile.gather(blocks, chosen, n * count, index_of, range(units), 2 * slots)
        mean = product(chosen, (own_half, other_half))
        for n, (_, name) in enumerate(wanted):
            pieces, flag, start = shards[name]
            for unit in range(units):
                for g in range(tile.tile_rows):
                    at = (unit * tile.tile_rows + g) * tile.group
                    field = tile.read(pieces, flag, row, unit + first - start, g)
                    value = field - mean[n * count + at : n * count + at + tile.group, :]
                    outs[n][at : at + tile.group, :] = value.astype(jnp.bfloat16)


def halo(tile, row, even, odd, unit, r):
    above = r < REACH
    g = (tile.split - REACH + r) if above else (r - REACH - tile.tile_rows)
    at = unit * tile.unit + g * tile.group
    from_even, from_odd = (p[at : at + tile.group, :].astype(jnp.float32) for p in (even, odd))
    return jnp.where((row % 2 == 0) == above, from_odd, from_even)


def edge_kernel(tile, parity, first, second, even, odd, out):
    row, col = lax.axis_index("rows"), lax.axis_index("cols")
    for r in range(tile.tile_rows + 2 * REACH):
        sides = []
        for unit in (0, tile.units - 1):
            g = r - REACH
            if 0 <= g < tile.tile_rows:
                sides.append(tile.read((first, second), 0, row, unit, g))
            else:
                sides.append(halo(tile, row, even, odd, unit, r))
        value = jnp.where(col % 2 == parity, sides[1], sides[0])
        out[r * tile.group : (r + 1) * tile.group, :] = value.astype(jnp.bfloat16)


def near_kernel(tile, slots, units, sides, ints_in, first, second, even, odd, *refs):
    *refs, ints, arrived = refs
    copy = pltpu.make_async_copy(ints_in, ints, arrived)
    copy.start()
    halos = refs[:sides]
    own_half, other_half, out, *refs = refs[sides:]
    factors, loads = (own_half, other_half), []
    if len(refs) > 2:
        *factors, blocks, chosen, factor_sem = refs
        for i, source in enumerate((own_half, other_half)):
            loads.append(pltpu.make_async_copy(source, factors[i], factor_sem.at[i]))
            loads[i].start()
    else:
        blocks, chosen = refs
    row, col = lax.axis_index("rows"), lax.axis_index("cols")
    above, below = row > 0, row < tile.rows - 1
    wide, last = tile.wide, tile.tile_rows + REACH
    nothing = jnp.zeros((REACH, tile.half, tile.pixels), jnp.float32)
    read = sorted({u + i for u in units for i in (-1, 0, 1)} & set(range(tile.units)))
    for r in range(last + REACH):
        inside = above if r < REACH else below if r >= last else None
        for unit in read:
            if inside is None:
                value = tile.read((first, second), 0, row, unit, r - REACH)
            else:
                value = jnp.where(inside, halo(tile, row, even, odd, unit, r), 0.0)
            blocks[pl.ds(r * wide + REACH + unit * REACH, REACH)] = tile.blocks(value)
        if not {0, tile.units - 1} & set(units):
            continue
        left, right = nothing, nothing
        for parity in range(sides):
            value = halos[parity][r * tile.group : (r + 1) * tile.group, :].astype(jnp.float32)
            if inside is not None:
                value = jnp.where(inside, value, 0.0)
            value = tile.blocks(value)
            on_right = col % 2 == parity
            right = jnp.where(on_right & (col < tile.cols - 1), value, right)
            left = jnp.where(jnp.logical_not(on_right) & (col > 0), value, left)
        blocks[pl.ds(r * wide, REACH)] = left
        blocks[pl.ds(r * wide + REACH + tile.tile_cols, REACH)] = right

    def index_of(g, j, k):
        return ints[g, k * tile.tile_cols + j]

    copy.wait()
    tile.gather(blocks, chosen, 0, index_of, units, 2 * slots)
    for load in loads:
        load.wait()
    mean = product(chosen, factors)
    for n, unit in enumerate(units):
        for g in range(tile.tile_rows):
            at = (n * tile.tile_rows + g) * tile.group
            value = tile.read((first, second), 0, row, unit, g)
            out[at : at + tile.group, :] = (value - mean[at : at + tile.group, :]).astype(jnp.bfloat16)


def mix_kernel(tile, parts, inner, outer, level_in, near_in, near_out, *refs):
    *refs, level, arrived = refs
    copy = pltpu.make_async_copy(level_in, level, arrived)
    copy.start()
    copy.wait()
    own, out, awaited = refs[: len(parts)], refs[-2], refs[-1]
    row = lax.axis_index("rows")
    at_end = (row == 0) | (row == tile.rows - 1)
    lower = lax.broadcasted_iota(jnp.int32, (tile.group, tile.pixels), 0) // tile.half
    first = 0
    for c, units in enumerate(parts):
        for unit in range(units):
            for g in range(tile.tile_rows):
                at = (unit * tile.tile_rows + g) * tile.group
                far = own[c][at : at + tile.group, :].astype(jnp.float32)
                near, n = near_in, inner.index(first + unit) if first + unit in inner else 0
                if first + unit in outer:
                    near, n = near_out, outer.index(first + unit)
                at = (n * tile.tile_rows + g) * tile.group
                fine = near[at : at + tile.group, :].astype(jnp.float32)
                levels = level[g, (first + unit) * REACH]
                for i in range(1, REACH):
                    levels = jnp.where(lower == i, level[g, (first + unit) * REACH + i], levels)
                at = (g * tile.units + first + unit) * tile.group
                mixed = jnp.where(levels == 1, fine, far)
                out[at : at + tile.group, :] = mixed.astype(jnp.bfloat16)
                wait = jnp.where((levels != 1) & at_end, 1.0, 0.0)
                awaited[at : at + tile.group, :] = wait.astype(jnp.bfloat16)
        first += units


def final_kernel(tile, parts, mixed, awaited, *refs):
    out = refs[-1]
    first = 0
    for c, units in enumerate(parts):
        for unit in range(units):
            for g in range(tile.tile_rows):
                at = (unit * tile.tile_rows + g) * tile.group
                at_out = (g * tile.units + first + unit) * tile.group
                spot = slice(at_out, at_out + tile.group)
                far = refs[c][at : at + tile.group, :].astype(jnp.float32)
                value = mixed[spot, :].astype(jnp.float32)
                value = jnp.where(awaited[spot, :].astype(jnp.float32) > 0.5, far, value)
                out[spot, :] = value.astype(jnp.bfloat16)
        first += units


def on_device(convergence, block_level, near_codes, far_rows, near_factor, far_factor):
    tile_rows, tile_cols, samples, pixels = convergence.shape
    rows, cols = lax.axis_size("rows"), lax.axis_size("cols")
    row, sub = lax.axis_index("rows"), lax.axis_index("sub")
    half = samples // lax.axis_size("sub")
    near_slots, far_slots = near_codes.shape[2], far_rows.shape[2]
    tile = Tile(rows, cols, tile_rows, tile_cols, half, pixels)
    parts = [tile.units * part // sum(PARTS) for part in PARTS]
    starts = [sum(parts[:c]) for c in range(len(parts))]

    own = []
    for later in (row % 2 == 0, row % 2 != 0):
        start = jnp.where(later, tile.split, 0)
        piece = lax.dynamic_slice(
            convergence, (start, 0, sub * half, 0), (tile.split, tile_cols, half, pixels)
        ).reshape(tile.split, tile.units, REACH, half, pixels)
        own.append(jnp.transpose(piece, (1, 0, 2, 3, 4)).reshape(-1, pixels))

    requests = jnp.transpose(far_rows, (0, 2, 1))
    partners = exchange(requests, "rows", 0)
    far_other = swap_sub(far_factor)
    near_other = swap_sub(near_factor)

    first = exchange(own[0], "rows", 0)
    side = exchange(own[1], "rows", 1)
    held = after(own, partners, far_other, near_other)
    even = [[first, exchange(held[1], "rows", 0)]]
    odd = [[side, exchange(held[0], "rows", 1)]]

    beside = [*own, even[0][0], odd[0][0]]
    edges = [
        call(
            functools.partial(edge_kernel, tile, parity),
            (tile_rows + 2 * REACH) * tile.group, pixels, [], beside, [],
        )[0]
        for parity in range(min(cols - 1, 2))
    ]
    halos = [exchange(edge, "cols", parity) for parity, edge in enumerate(edges)]

    near_index = jnp.transpose(near_codes, (0, 2, 1))
    near_index = near_index + (tile.wide - 2 * REACH - 1) * (near_index // (2 * REACH + 1))
    near_index = near_index + tile.wide * jnp.arange(tile_rows, dtype=jnp.int32)[:, None, None]
    near_index = near_index + jnp.arange(tile_cols, dtype=jnp.int32)[None, None, :]
    codes = jnp.concatenate([near_index, requests, partners], axis=1)
    other = swap_sub(codes)
    near_ints = jnp.concatenate([near_index, other[:, :near_slots]], axis=1)
    far_ints = jnp.concatenate([codes[:, near_slots:], other[:, near_slots:]], axis=1)
    near_ints, far_ints = (x.reshape(tile_rows, -1) for x in (near_ints, far_ints))

    size = tile_rows * tile_cols * half
    inner_units, outer_units = list(range(1, tile.units - 1)), [0, tile.units - 1]

    def near_part(units, sides, factors, bring):
        count = tile_rows * len(units) * tile.group
        scratch = [
            pltpu.VMEM(((tile_rows + 2 * REACH) * tile.wide, half, pixels), jnp.float32),
            pltpu.VMEM((count, 2 * near_slots * pixels), jnp.bfloat16),
        ]
        return call(
            functools.partial(near_kernel, tile, near_slots, units, len(sides)),
            count, pixels, [near_ints], [*beside, *sides, *factors],
            scratch + [pltpu.SemaphoreType.DMA((2,))] * bring,
            left=2 * bring,
            more=[jax.ShapeDtypeStruct(x.shape, x.dtype) for x in factors] * bring,
        )

    near_inner, *brought = near_part(inner_units, [], [near_factor, near_other], 1)
    (near_outer,) = near_part(outer_units, halos, brought, 0)

    inner = rows > 4
    for step in range(1, rows - 3):
        if inner:
            even.append([exchange(x, "rows", 0) for x in odd[step - 1]])
        odd.append([exchange(x, "rows", 1) for x in even[step - 1]])
    source = after(even[rows - 4], near_inner, far_ints, *halos, odd[0][1])
    def cut(pieces, c):
        spots = slice(starts[c] * tile.unit, (starts[c] + parts[c]) * tile.unit)
        return jnp.concatenate([x[spots] for x in pieces], axis=0)

    last = [exchange(cut(source, c), "rows", 1) for c in range(len(parts))]

    def far_chunk(c, wanted, *before):
        names, arrays = [((0, -1), 0, None)], [*own]
        for step in range(len(odd)):
            if step < len(even):
                names.append(((0, step), 1, None))
                arrays += even[step]
            names.append(((1, step), 0, None))
            arrays += odd[step]
        names.append(((1, len(odd)), 0, starts[c]))
        arrays.append(last[c])
        if before:
            arrays = list(after(arrays[:1], *before)) + arrays[1:]
        here = tile_rows * parts[c] * tile.group
        return call(
            functools.partial(
                far_kernel, tile, names, starts[c], parts[c], wanted, far_slots
            ),
            here, pixels, [far_ints], [*arrays, far_factor, far_other],
            [
                pltpu.VMEM(((rows + 1) * tile_rows * parts[c] * REACH, half, pixels), jnp.float32),
                pltpu.VMEM((len(wanted) * here, 2 * far_slots * pixels), jnp.bfloat16),
            ],
            len(wanted),
        )

    slots = [k + 2 * far_slots * s for s in range(2) for k in range(far_slots)]
    partner = ([far_slots + k for k in slots], (0, 0))
    mine = (slots, (0, -1))
    ready = []
    sent = near_outer
    for c in range(len(parts)):
        (sent,) = far_chunk(c, [partner], sent)
        ready.append(exchange(sent, "rows", 0))
    far_own = [far_chunk(c, [mine], sent)[0] for c in range(len(parts))]
    mixed, awaited = call(
        functools.partial(mix_kernel, tile, parts, inner_units, outer_units),
        size, pixels, [block_level], [near_inner, near_outer, *far_own], [], 2,
    )
    (result,) = call(
        functools.partial(final_kernel, tile, parts),
        size, pixels, [], [mixed, awaited, *ready], [],
    )
    return result.reshape(tile_rows, tile_cols, half, pixels)


def solution(mesh):
    placed = (
        P(("fields", "rows"), "cols", None, None),
        P(("fields", "rows"), "cols"),
        P(("fields", "rows"), "cols", "sub"),
        P(("fields", "rows"), "cols", "sub"),
        P(None, "sub"),
        P(None, "sub"),
    )
    return jax.shard_map(
        on_device,
        mesh=mesh,
        in_specs=placed,
        out_specs=P(("fields", "rows"), "cols", "sub", None),
        check_vma=False,
    )
```

```python
import functools

import jax
import jax.numpy as jnp
from jax import lax
from jax.experimental import pallas as pl
from jax.experimental.pallas import tpu as pltpu
from jax.sharding import PartitionSpec as P

REACH = 2
PARTS = (3, 3, 2)
VMEM_BYTES = 48 * 2**20
CONTRACT_LAST = (((1,), (1,)), ((), ()))


def exchange(array, axis, parity):
    count, subs = lax.axis_size(axis), lax.axis_size("sub")
    partner = list(range(count))
    for i in range(parity, count - 1, 2):
        partner[i], partner[i + 1] = i + 1, i
    pairs = []
    for i in range(count):
        for s in range(subs):
            other = s if partner[i] != i else subs - 1 - s
            pairs.append((i * subs + s, partner[i] * subs + other))
    return lax.ppermute(array, (axis, "sub"), pairs)


def swap_sub(array):
    subs = lax.axis_size("sub")
    return lax.ppermute(array, "sub", [(s, subs - 1 - s) for s in range(subs)])


def after(arrays, *first):
    return lax.optimization_barrier((tuple(arrays), first))[0]


def call(kernel, rows, pixels, ints, arrays, scratch, outputs=1, left=0, more=()):
    shape = jax.ShapeDtypeStruct((rows, pixels), jnp.bfloat16)
    vmem = pl.BlockSpec(memory_space=pltpu.VMEM)
    return pl.pallas_call(
        kernel,
        out_shape=[shape] * outputs + list(more),
        in_specs=[vmem] * (len(ints) + len(arrays) - left)
        + [pl.BlockSpec(memory_space=pltpu.HBM)] * left,
        out_specs=[vmem] * (outputs + len(more)),
        scratch_shapes=scratch
        + [pltpu.SMEM(x.shape, x.dtype) for x in ints]
        + [pltpu.SemaphoreType.DMA] * len(ints),
        compiler_params=pltpu.CompilerParams(vmem_limit_bytes=VMEM_BYTES),
    )(*ints, *arrays)


class Tile:
    def __init__(self, rows, cols, tile_rows, tile_cols, half, pixels):
        self.rows, self.cols = rows, cols
        self.tile_rows, self.tile_cols = tile_rows, tile_cols
        self.half, self.pixels = half, pixels
        self.split = tile_rows // 2
        self.units = tile_cols // REACH
        self.group = REACH * half
        self.unit = self.split * self.group
        self.wide = tile_cols + 2 * REACH

    def read(self, pieces, flag, row, unit, g):
        at = unit * self.unit + (g % self.split) * self.group
        first, second = (p[at : at + self.group, :].astype(jnp.float32) for p in pieces)
        later = row % 2 == flag
        return jnp.where(later, *((first, second) if g >= self.split else (second, first)))

    def blocks(self, value):
        return value.reshape(REACH, self.half, self.pixels)

    def gather(self, blocks, chosen, base, index_of, units, slots):
        def one_row(g, carry):
            for n, unit in enumerate(units):
                at = pl.multiple_of(base + (n * self.tile_rows + g) * self.group, self.group)
                for k in range(slots):
                    pair = [blocks[index_of(g, unit * REACH + i, k)] for i in range(REACH)]
                    chosen[pl.ds(at, self.group), k * self.pixels : (k + 1) * self.pixels] = (
                        jnp.concatenate(pair, axis=0).astype(jnp.bfloat16)
                    )
            return carry

        lax.fori_loop(0, self.tile_rows, one_row, 0)


def product(chosen, factors):
    total = None
    start = 0
    for factor in factors:
        depth = factor.shape[1]
        term = lax.dot_general(
            chosen[:, start : start + depth], factor[...], CONTRACT_LAST,
            preferred_element_type=jnp.float32,
        )
        total = term if total is None else total + term
        start += depth
    return total


def far_kernel(tile, names, first, units, wanted, slots, ints_in, *refs):
    *refs, ints, arrived = refs
    row = lax.axis_index("rows")

    @pl.when((row > 0) & (row < tile.rows - 1))
    def _():
        copy = pltpu.make_async_copy(ints_in, ints, arrived)
        copy.start()
        sign = jnp.where(row % 2 == 0, 1, -1)
        width = units * REACH
        shards = {}
        taken = 0
        size = units * tile.unit
        for name, flag, start in names:
            if start is None:
                shards[name] = (refs[taken : taken + 2], flag, 0)
                taken += 2
            else:
                pieces = [refs[taken].at[pl.ds(at, size), :] for at in (0, size)]
                shards[name] = (pieces, flag, start)
                taken += 1
        own_half, other_half, *outs = refs[taken : taken + 2 + len(wanted)]
        blocks, chosen = refs[taken + 2 + len(wanted) :]
        for (parity, step), (pieces, flag, start) in shards.items():
            away = 0 if step < 0 else (1 + step) * (sign if parity == 0 else -sign)
            source = row + away
            source = jnp.where((source >= 0) & (source < tile.rows), source, tile.rows)
            for half, piece in enumerate(pieces):
                later = (row % 2 == flag) == (half == 0)
                base = source * tile.tile_rows + jnp.where(later, tile.split, 0)
                for unit in range(units):
                    for g in range(tile.split):
                        at = (unit + first - start) * tile.unit + g * tile.group
                        value = piece[at : at + tile.group, :].astype(jnp.float32)
                        blocks[pl.ds((base + g) * width + unit * REACH, REACH)] = tile.blocks(value)

        copy.wait()
        count = tile.tile_rows * units * tile.group
        for n, (plane, _) in enumerate(wanted):

            def index_of(g, j, k):
                return ints[g, plane[k] * tile.tile_cols + first * REACH + j] * width + j

            tile.gather(blocks, chosen, n * count, index_of, range(units), 2 * slots)
        mean = product(chosen, (own_half, other_half))
        for n, (_, name) in enumerate(wanted):
            pieces, flag, start = shards[name]
            for unit in range(units):
                for g in range(tile.tile_rows):
                    at = (unit * tile.tile_rows + g) * tile.group
                    field = tile.read(pieces, flag, row, unit + first - start, g)
                    value = field - mean[n * count + at : n * count + at + tile.group, :]
                    outs[n][at : at + tile.group, :] = value.astype(jnp.bfloat16)


def halo(tile, row, even, odd, unit, r):
    above = r < REACH
    g = (tile.split - REACH + r) if above else (r - REACH - tile.tile_rows)
    at = unit * tile.unit + g * tile.group
    from_even, from_odd = (p[at : at + tile.group, :].astype(jnp.float32) for p in (even, odd))
    return jnp.where((row % 2 == 0) == above, from_odd, from_even)


def edge_kernel(tile, parity, first, second, even, odd, out):
    row, col = lax.axis_index("rows"), lax.axis_index("cols")
    for r in range(tile.tile_rows + 2 * REACH):
        sides = []
        for unit in (0, tile.units - 1):
            g = r - REACH
            if 0 <= g < tile.tile_rows:
                sides.append(tile.read((first, second), 0, row, unit, g))
            else:
                sides.append(halo(tile, row, even, odd, unit, r))
        value = jnp.where(col % 2 == parity, sides[1], sides[0])
        out[r * tile.group : (r + 1) * tile.group, :] = value.astype(jnp.bfloat16)


def near_kernel(tile, slots, units, sides, ints_in, first, second, even, odd, *refs):
    *refs, ints, arrived = refs
    copy = pltpu.make_async_copy(ints_in, ints, arrived)
    copy.start()
    halos = refs[:sides]
    own_half, other_half, out, *refs = refs[sides:]
    factors, loads = (own_half, other_half), []
    if len(refs) > 2:
        *factors, blocks, chosen, factor_sem = refs
        for i, source in enumerate((own_half, other_half)):
            loads.append(pltpu.make_async_copy(source, factors[i], factor_sem.at[i]))
            loads[i].start()
    else:
        blocks, chosen = refs
    row, col = lax.axis_index("rows"), lax.axis_index("cols")
    above, below = row > 0, row < tile.rows - 1
    wide, last = tile.wide, tile.tile_rows + REACH
    nothing = jnp.zeros((REACH, tile.half, tile.pixels), jnp.float32)
    read = sorted({u + i for u in units for i in (-1, 0, 1)} & set(range(tile.units)))
    for r in range(last + REACH):
        inside = above if r < REACH else below if r >= last else None
        for unit in read:
            if inside is None:
                value = tile.read((first, second), 0, row, unit, r - REACH)
            else:
                value = jnp.where(inside, halo(tile, row, even, odd, unit, r), 0.0)
            blocks[pl.ds(r * wide + REACH + unit * REACH, REACH)] = tile.blocks(value)
        if not {0, tile.units - 1} & set(units):
            continue
        left, right = nothing, nothing
        for parity in range(sides):
            value = halos[parity][r * tile.group : (r + 1) * tile.group, :].astype(jnp.float32)
            if inside is not None:
                value = jnp.where(inside, value, 0.0)
            value = tile.blocks(value)
            on_right = col % 2 == parity
            right = jnp.where(on_right & (col < tile.cols - 1), value, right)
            left = jnp.where(jnp.logical_not(on_right) & (col > 0), value, left)
        blocks[pl.ds(r * wide, REACH)] = left
        blocks[pl.ds(r * wide + REACH + tile.tile_cols, REACH)] = right

    def index_of(g, j, k):
        return ints[g, k * tile.tile_cols + j]

    copy.wait()
    tile.gather(blocks, chosen, 0, index_of, units, 2 * slots)
    for load in loads:
        load.wait()
    mean = product(chosen, factors)
    for n, unit in enumerate(units):
        for g in range(tile.tile_rows):
            at = (n * tile.tile_rows + g) * tile.group
            value = tile.read((first, second), 0, row, unit, g)
            out[at : at + tile.group, :] = (value - mean[at : at + tile.group, :]).astype(jnp.bfloat16)


def mix_kernel(tile, parts, inner, outer, level_in, near_in, near_out, *refs):
    *refs, level, arrived = refs
    copy = pltpu.make_async_copy(level_in, level, arrived)
    copy.start()
    copy.wait()
    own, (out, awaited, whole, stored) = refs[: len(parts)], refs[len(parts) :]
    row = lax.axis_index("rows")
    at_end = (row == 0) | (row == tile.rows - 1)
    lower = lax.broadcasted_iota(jnp.int32, (tile.group, tile.pixels), 0) // tile.half
    first = 0
    for c, units in enumerate(parts):
        for unit in range(units):
            for g in range(tile.tile_rows):
                at = (unit * tile.tile_rows + g) * tile.group
                far = own[c][at : at + tile.group, :].astype(jnp.float32)
                near, n = near_in, inner.index(first + unit) if first + unit in inner else 0
                if first + unit in outer:
                    near, n = near_out, outer.index(first + unit)
                at = (n * tile.tile_rows + g) * tile.group
                fine = near[at : at + tile.group, :].astype(jnp.float32)
                levels = level[g, (first + unit) * REACH]
                for i in range(1, REACH):
                    levels = jnp.where(lower == i, level[g, (first + unit) * REACH + i], levels)
                at = (g * tile.units + first + unit) * tile.group
                mixed = jnp.where(levels == 1, fine, far)
                out[at : at + tile.group, :] = mixed.astype(jnp.bfloat16)
                wait = jnp.where((levels != 1) & at_end, 1.0, 0.0)
                awaited[at : at + tile.group, :] = wait.astype(jnp.bfloat16)
        first += units
    store = pltpu.make_async_copy(out, whole, stored)
    store.start()
    store.wait()


def final_kernel(tile, parts, first, mixed, awaited, *refs):
    ready, (_, out, chosen, done) = refs[: len(parts)], refs[len(parts) :]
    row = lax.axis_index("rows")

    @pl.when((row == 0) | (row == tile.rows - 1))
    def _():
        span = sum(parts) * tile.group
        copies = []
        for g in range(tile.tile_rows):
            begin = (g * tile.units + first) * tile.group
            shift = 0
            for c, units in enumerate(parts):
                for unit in range(units):
                    at = (unit * tile.tile_rows + g) * tile.group
                    spot = slice(begin + shift, begin + shift + tile.group)
                    far = ready[c][at : at + tile.group, :].astype(jnp.float32)
                    value = mixed[spot, :].astype(jnp.float32)
                    value = jnp.where(awaited[spot, :].astype(jnp.float32) > 0.5, far, value)
                    at = g * span + shift
                    chosen[at : at + tile.group, :] = value.astype(jnp.bfloat16)
                    shift += tile.group
            part = chosen.at[pl.ds(g * span, span), :]
            copies.append(pltpu.make_async_copy(part, out.at[pl.ds(begin, span), :], done.at[g]))
            copies[g].start()
        for copy in copies:
            copy.wait()


def on_device(convergence, block_level, near_codes, far_rows, near_factor, far_factor):
    tile_rows, tile_cols, samples, pixels = convergence.shape
    rows, cols = lax.axis_size("rows"), lax.axis_size("cols")
    row, sub = lax.axis_index("rows"), lax.axis_index("sub")
    half = samples // lax.axis_size("sub")
    near_slots, far_slots = near_codes.shape[2], far_rows.shape[2]
    tile = Tile(rows, cols, tile_rows, tile_cols, half, pixels)
    parts = [tile.units * part // sum(PARTS) for part in PARTS]
    starts = [sum(parts[:c]) for c in range(len(parts))]

    own = []
    for later in (row % 2 == 0, row % 2 != 0):
        start = jnp.where(later, tile.split, 0)
        piece = lax.dynamic_slice(
            convergence, (start, 0, sub * half, 0), (tile.split, tile_cols, half, pixels)
        ).reshape(tile.split, tile.units, REACH, half, pixels)
        own.append(jnp.transpose(piece, (1, 0, 2, 3, 4)).reshape(-1, pixels))

    requests = jnp.transpose(far_rows, (0, 2, 1))
    partners = exchange(requests, "rows", 0)
    far_other = swap_sub(far_factor)
    near_other = swap_sub(near_factor)

    first = exchange(own[0], "rows", 0)
    side = exchange(own[1], "rows", 1)
    held = after(own, partners, far_other, near_other)
    even = [[first, exchange(held[1], "rows", 0)]]
    odd = [[side, exchange(held[0], "rows", 1)]]

    beside = [*own, even[0][0], odd[0][0]]
    edges = [
        call(
            functools.partial(edge_kernel, tile, parity),
            (tile_rows + 2 * REACH) * tile.group, pixels, [], beside, [],
        )[0]
        for parity in range(min(cols - 1, 2))
    ]
    halos = [exchange(edge, "cols", parity) for parity, edge in enumerate(edges)]

    near_index = jnp.transpose(near_codes, (0, 2, 1))
    near_index = near_index + (tile.wide - 2 * REACH - 1) * (near_index // (2 * REACH + 1))
    near_index = near_index + tile.wide * jnp.arange(tile_rows, dtype=jnp.int32)[:, None, None]
    near_index = near_index + jnp.arange(tile_cols, dtype=jnp.int32)[None, None, :]
    codes = jnp.concatenate([near_index, requests, partners], axis=1)
    other = swap_sub(codes)
    near_ints = jnp.concatenate([near_index, other[:, :near_slots]], axis=1)
    far_ints = jnp.concatenate([codes[:, near_slots:], other[:, near_slots:]], axis=1)
    near_ints, far_ints = (x.reshape(tile_rows, -1) for x in (near_ints, far_ints))

    size = tile_rows * tile_cols * half
    inner_units, outer_units = list(range(1, tile.units - 1)), [0, tile.units - 1]

    def near_part(units, sides, factors, bring):
        count = tile_rows * len(units) * tile.group
        scratch = [
            pltpu.VMEM(((tile_rows + 2 * REACH) * tile.wide, half, pixels), jnp.float32),
            pltpu.VMEM((count, 2 * near_slots * pixels), jnp.bfloat16),
        ]
        return call(
            functools.partial(near_kernel, tile, near_slots, units, len(sides)),
            count, pixels, [near_ints], [*beside, *sides, *factors],
            scratch + [pltpu.SemaphoreType.DMA((2,))] * bring,
            left=2 * bring,
            more=[jax.ShapeDtypeStruct(x.shape, x.dtype) for x in factors] * bring,
        )

    near_inner, *brought = near_part(inner_units, [], [near_factor, near_other], 1)
    (near_outer,) = near_part(outer_units, halos, brought, 0)

    inner = rows > 4
    for step in range(1, rows - 3):
        if inner:
            even.append([exchange(x, "rows", 0) for x in odd[step - 1]])
        odd.append([exchange(x, "rows", 1) for x in even[step - 1]])
    source = after(even[rows - 4], near_inner, far_ints, *halos, odd[0][1])
    def cut(pieces, c):
        spots = slice(starts[c] * tile.unit, (starts[c] + parts[c]) * tile.unit)
        return jnp.concatenate([x[spots] for x in pieces], axis=0)

    last = [exchange(cut(source, c), "rows", 1) for c in range(len(parts))]

    def far_chunk(c, wanted, *before):
        names, arrays = [((0, -1), 0, None)], [*own]
        for step in range(len(odd)):
            if step < len(even):
                names.append(((0, step), 1, None))
                arrays += even[step]
            names.append(((1, step), 0, None))
            arrays += odd[step]
        names.append(((1, len(odd)), 0, starts[c]))
        arrays.append(last[c])
        if before:
            arrays = list(after(arrays[:1], *before)) + arrays[1:]
        here = tile_rows * parts[c] * tile.group
        return call(
            functools.partial(
                far_kernel, tile, names, starts[c], parts[c], wanted, far_slots
            ),
            here, pixels, [far_ints], [*arrays, far_factor, far_other],
            [
                pltpu.VMEM(((rows + 1) * tile_rows * parts[c] * REACH, half, pixels), jnp.float32),
                pltpu.VMEM((len(wanted) * here, 2 * far_slots * pixels), jnp.bfloat16),
            ],
            len(wanted),
        )

    slots = [k + 2 * far_slots * s for s in range(2) for k in range(far_slots)]
    partner = ([far_slots + k for k in slots], (0, 0))
    mine = (slots, (0, -1))
    ready = []
    sent = near_outer
    for c in range(len(parts)):
        (sent,) = far_chunk(c, [partner], sent)
        ready.append(exchange(sent, "rows", 0))
    far_own = [far_chunk(c, [mine], sent)[0] for c in range(len(parts))]
    vmem, hbm = (pl.BlockSpec(memory_space=space) for space in (pltpu.VMEM, pltpu.HBM))
    params = pltpu.CompilerParams(vmem_limit_bytes=VMEM_BYTES)
    shape = jax.ShapeDtypeStruct((size, pixels), jnp.bfloat16)
    mixed, awaited, result = pl.pallas_call(
        functools.partial(mix_kernel, tile, parts, inner_units, outer_units),
        out_shape=[shape] * 3,
        in_specs=[vmem] * (3 + len(parts)),
        out_specs=[vmem, vmem, hbm],
        scratch_shapes=[
            pltpu.SemaphoreType.DMA,
            pltpu.SMEM(block_level.shape, block_level.dtype),
            pltpu.SemaphoreType.DMA,
        ],
        compiler_params=params,
    )(block_level, near_inner, near_outer, *far_own)
    for some in (range(len(parts) - 1), range(len(parts) - 1, len(parts))):
        units = [parts[c] for c in some]
        result = pl.pallas_call(
            functools.partial(final_kernel, tile, units, starts[some[0]]),
            out_shape=shape,
            in_specs=[vmem] * (2 + len(units)) + [hbm],
            out_specs=hbm,
            scratch_shapes=[
                pltpu.VMEM((tile_rows * sum(units) * tile.group, pixels), jnp.bfloat16),
                pltpu.SemaphoreType.DMA((tile_rows,)),
            ],
            input_output_aliases={2 + len(units): 0},
            compiler_params=params,
        )(mixed, awaited, *(ready[c] for c in some), result)
    return result.reshape(tile_rows, tile_cols, half, pixels)


def solution(mesh):
    placed = (
        P(("fields", "rows"), "cols", None, None),
        P(("fields", "rows"), "cols"),
        P(("fields", "rows"), "cols", "sub"),
        P(("fields", "rows"), "cols", "sub"),
        P(None, "sub"),
        P(None, "sub"),
    )
    return jax.shard_map(
        on_device,
        mesh=mesh,
        in_specs=placed,
        out_specs=P(("fields", "rows"), "cols", "sub", None),
        check_vma=False,
    )
```
